32 devices in a mesh: run: 2 (over y), spec: 16 (over z, x, core).
Axes of the slice: x: 2, y: 2, z: 4, core: 2. Of those that a mesh axis runs over, the one named last changes fastest.
Arguments:
- tensor: bfloat16 [8, 2048, 8192], P('run', None, 'spec'), may hold values from -6 to 6
- run_factor: float32 [8, 64], P('run'), may hold values from -0.0625 to 0.0625
- mz_factor: float32 [8192, 64], P('spec'), may hold values from -6 to 6
Outputs:
- rt_factor: float32 [2048, 64], P('spec')
- mz_out: float32 [8192, 64], P('spec')
The draws below stay inside these ranges and needn't reach their ends.
All inputs are finite; a program needn't handle non-finite values.
Results may differ from the reference program's by a relative error of at most 0.0052.
Values may be sent and summed in bfloat16 or wider, within the bound.
A program may use at most 64 MiB of HBM per device.

```python
import jax
import jax.numpy as jnp
from jax import lax

RT = 2048
RANK = 64
SWEEPS = 3
RUNS = 8
MZ = 8192


def with_spikes(entries, stream_key, source, target, blocks, factor):
    owner, partner = [(jnp.arange(entries.shape[dim]) // (entries.shape[dim] // blocks)).reshape([-1 if axis == dim else 1 for axis in range(entries.ndim)]) for dim in (source, target)]
    chosen = jax.random.permutation(stream_key, blocks)[partner]
    strong = (owner == chosen) | (owner == (partner + blocks // 2) % blocks)
    return jnp.where(strong, factor * entries, entries)


def level_of(rng, extent, shards, least, high):
    def one(dim, blocks):
        steps = jax.random.uniform(jax.random.fold_in(jax.random.fold_in(rng, 6), dim), (blocks,), jnp.float32, least / len(shards), high / len(shards))
        return jnp.repeat(jnp.exp(steps), extent[dim] // blocks).reshape((-1,) + (1,) * (len(extent) - dim - 1))

    factor_of = one(*shards[0])
    for cut in shards[1:]:
        factor_of = factor_of * one(*cut)
    return factor_of


def noise(own_key, shape, spread, most, cuts=(), dtype=jnp.bfloat16):
    level = level_of(own_key, shape, cuts, -0.22, 0.18) if cuts else 1.0
    drawn = jax.random.normal(own_key, shape, jnp.float32) * spread * level
    return jnp.minimum(jnp.maximum(drawn, -most), most).astype(dtype)


def noise_with(rng, extent, width, bound, pieces, heavy, dtype=jnp.bfloat16):
    result = width * jax.random.normal(rng, extent, jnp.float32)
    if pieces:
        result = result * level_of(rng, extent, pieces, -0.22, 0.18)
    return jnp.clip(with_spikes(result, jax.random.fold_in(rng, 3), *heavy), -bound, bound).astype(dtype)


def setup_inputs(seed: int = 0) -> dict:
    keys = jax.random.split(jax.random.key(seed), 4)
    tensor = noise_with(keys[0], (RUNS, RT, MZ), 1.0, 6.0, ((0, 2), (2, 16)), (2, 1, 16, 2.0))
    run_factor = noise(keys[1], (RUNS, RANK), (1.0 / (RUNS * MZ) ** 0.5), 0.0625, ((0, 2),), jnp.float32)
    mz_factor = noise(keys[2], (MZ, RANK), 1.0, 6.0, ((0, 16),), jnp.float32)
    return dict(tensor=tensor, run_factor=run_factor, mz_factor=mz_factor)


def solve_rows(gram, moment):
    return jnp.linalg.solve(gram, moment.T).T

def reference(tensor, run_factor, mz_factor):
    highest = lax.Precision.HIGHEST
    run_gram = jnp.dot(run_factor.T, run_factor, precision=highest)
    mz_now = mz_factor
    rt_factor = jnp.zeros((RT, RANK), jnp.float32)
    for sweep_index in range(SWEEPS):
        mz_gram = jnp.dot(mz_now.T, mz_now, precision=highest)
        mz_half = mz_now.astype(jnp.bfloat16)

        def rt_step(total, inputs):
            slab, weights = inputs
            proj = jnp.dot(slab.astype(jnp.float32), mz_half.astype(jnp.float32), preferred_element_type=jnp.float32)
            return (total + weights[None, :] * proj, None)
        rt_moment, unused = lax.scan(rt_step, jnp.zeros((RT, RANK), jnp.float32), (tensor, run_factor))
        rt_factor = solve_rows(run_gram * mz_gram, rt_moment)
        rt_gram = jnp.dot(rt_factor.T, rt_factor, precision=highest)
        rt_half = rt_factor.astype(jnp.bfloat16)

        def mz_step(total, inputs):
            slab, weights = inputs
            back = jnp.dot(slab.T.astype(jnp.float32), rt_half.astype(jnp.float32), preferred_element_type=jnp.float32)
            return (total + weights[None, :] * back, None)
        mz_moment, unused = lax.scan(mz_step, jnp.zeros((MZ, RANK), jnp.float32), (tensor, run_factor))
        mz_now = solve_rows(run_gram * rt_gram, mz_moment)
    return (rt_factor, mz_now)
```

```python
import functools

import jax
import jax.numpy as jnp
from jax import lax
from jax.experimental import pallas as pl
from jax.experimental.pallas import tpu as pltpu
from jax.sharding import PartitionSpec as P

SWEEPS = 3
ZDIM = 4
PARTS = 2
HIGHEST = lax.Precision.HIGHEST
F32 = jnp.float32
BF16 = jnp.bfloat16
NT = (((1,), (1,)), ((), ()))
TN = (((0,), (0,)), ((), ()))


def negative_inverse(a):
    n = a.shape[0]
    lanes = lax.broadcasted_iota(jnp.int32, (1, n), 1)
    rows = lax.broadcasted_iota(jnp.int32, (n, 1), 0)
    for p in range(n):
        col = a[:, p : p + 1]
        row = a[p : p + 1, :]
        inv = 1.0 / a[p : p + 1, p : p + 1]
        here = lanes == p
        scaled = jnp.where(here, 0.0, row * inv)
        keep = jnp.where(here, 0.0, a)
        swept = keep - col * scaled + jnp.where(here, col * inv, 0.0)
        pivot_row = scaled + jnp.where(here, -inv, 0.0)
        a = jnp.where(rows == p, pivot_row, swept)
    return a


def kernel(
    runs, xdim, t_hbm, rf_ref, rft_ref, mz_in, rt_out, mz_out,
    t_ref, mz_ref, half_ref, w_ref, rf_all, gram_own, gram_a, gram_sum, gram_b,
    mom, mom_c, red_c, mom_x, red_x, mom_z, mom_r, rt_all, mzs,
    load_sem, rf_sem, ga_sem, gb_sem, c_sem, x_sem, z_sem, r_sem, az_sem, ax_sem, ac_sem, m_sem,
):
    r = lax.axis_index("run")
    s = lax.axis_index("spec")
    c = lax.rem(s, 2)
    x = lax.rem(s // 2, xdim)
    z = s // (2 * xdim)
    local_runs, width = t_ref.shape[0], rt_out.shape[1]
    rank, mz_rows = mz_in.shape
    part = mz_rows // PARTS

    load = pltpu.make_async_copy(t_hbm, t_ref, load_sem)
    load.start()

    core_peer = s + 1 - 2 * c
    x_peers = [(lax.rem(x + d, xdim) - x) * 2 + s for d in range(1, xdim)]
    z_peers = [(lax.rem(z + d, ZDIM) - z) * 2 * xdim + s for d in range(1, ZDIM)]
    run_peers = [lax.rem(r + d, runs) for d in range(1, runs)]
    inner = lax.rem(s, 2 * xdim)
    inner_peers = [s - inner + lax.rem(inner + d, 2 * xdim) for d in range(1, 2 * xdim)]

    everyone = [(r, q) for q in inner_peers + z_peers] + [(q, s) for q in run_peers]
    barrier = pltpu.get_barrier_semaphore()
    for peer in everyone:
        pl.semaphore_signal(barrier, inc=1, device_id=peer, device_id_type=pl.DeviceIdType.MESH)
    pl.semaphore_wait(barrier, len(everyone))

    def send(src, dst, sems, index, peer):
        copy = pltpu.make_async_remote_copy(
            src_ref=src, dst_ref=dst, send_sem=sems.at[(0,) + index], recv_sem=sems.at[(1,) + index],
            device_id=peer, device_id_type=pl.DeviceIdType.MESH,
        )
        copy.start()
        return copy

    rf_all[r] = rf_ref[...]
    rf_copies = [send(rf_all.at[r], rf_all.at[r], rf_sem, (d,), (q, s)) for d, q in enumerate(run_peers)]
    mz_ref[...] = mz_in[...]
    for i in range(local_runs):
        w_ref[i] = jnp.broadcast_to(rft_ref[:, i : i + 1], w_ref.shape[1:])
    for copy in rf_copies:
        copy.wait()
    run_gram = jnp.zeros((rank, rank), F32)
    for i in range(runs):
        run_gram += lax.dot_general(rf_all[i], rf_all[i], TN, precision=HIGHEST, preferred_element_type=F32)
    load.wait()

    def sweep(n, run_gram):
        mz_now = mz_ref[...]
        gram_own[n] = lax.dot_general(mz_now, mz_now, NT, precision=HIGHEST, preferred_element_type=F32)
        ga = [send(gram_own.at[n], gram_a.at[n, d], ga_sem, (n, d), (r, q)) for d, q in enumerate(inner_peers)]
        half_ref[...] = mz_now.astype(BF16)

        def project(cc):
            for xx in range(xdim):
                for zz in range(0, ZDIM, 2):
                    total = jnp.zeros((rank, 2 * width), F32)
                    starts = [
                        pl.multiple_of((((zz + e) * xdim + xx) * 2 + cc) * width, width) for e in range(2)
                    ]
                    for i in range(local_runs):
                        slab = jnp.concatenate([t_ref[i, pl.ds(at, width), :] for at in starts], axis=0)
                        proj = lax.dot_general(half_ref[...], slab, NT, preferred_element_type=F32)
                        total += proj * jnp.concatenate([w_ref[i][:, :width]] * 2, axis=1)
                    mom[n, cc, xx, zz] = total[:, :width]
                    mom[n, cc, xx, zz + 1] = total[:, width:]

        project(1 - c)
        to_core = send(mom.at[n, 1 - c], mom_c.at[n], c_sem, (n,), (r, core_peer))
        project(c)
        for copy in ga:
            copy.wait()
        total = gram_own[n]
        for d in range(len(ga)):
            total += gram_a[n, d]
        gram_sum[n] = total
        gb = [send(gram_sum.at[n], gram_b.at[n, d], gb_sem, (n, d), (r, q)) for d, q in enumerate(z_peers)]
        to_core.wait()
        red_c[n] = mom[n, c] + mom_c[n]
        to_x = []
        for d, q in enumerate(x_peers):
            to_x.append(send(red_c.at[n, lax.rem(x + d + 1, xdim)], mom_x.at[n, d], x_sem, (n, d), (r, q)))
        for copy in gb:
            copy.wait()
        total = gram_sum[n]
        for d in range(len(gb)):
            total += gram_b[n, d]
        inverse = negative_inverse(run_gram * total)
        for copy in to_x:
            copy.wait()
        total = red_c[n, x]
        for d in range(len(to_x)):
            total += mom_x[n, d]
        red_x[n] = total
        to_z = []
        for d, q in enumerate(z_peers):
            to_z.append(send(red_x.at[n, lax.rem(z + d + 1, ZDIM)], mom_z.at[n, d], z_sem, (n, d), (r, q)))
        for copy in to_z:
            copy.wait()
        total = red_x[n, z]
        for d in range(len(to_z)):
            total += mom_z[n, d]
        mom_r[n, r] = total
        to_r = [send(mom_r.at[n, r], mom_r.at[n, r], r_sem, (n, d), (q, s)) for d, q in enumerate(run_peers)]
        for copy in to_r:
            copy.wait()
        total = mom_r[n, 0]
        for d in range(1, runs):
            total += mom_r[n, d]
        rt = -jnp.dot(inverse, total, precision=HIGHEST, preferred_element_type=F32)
        rt_out[...] = rt

        rt_all[n, c, x, z] = rt.astype(BF16)
        own = rt_all.at[n, c, x, z]
        copies = [send(own, own, az_sem, (n, d), (r, q)) for d, q in enumerate(z_peers)]
        for copy in copies:
            copy.wait()
        own = rt_all.at[n, c, x]
        copies = [send(own, own, ax_sem, (n, d), (r, q)) for d, q in enumerate(x_peers)]
        for copy in copies:
            copy.wait()
        own = rt_all.at[n, c]
        send(own, own, ac_sem, (n,), (r, core_peer)).wait()
        rt_half = jnp.concatenate(
            [rt_all[n, p % 2, p // 2 % xdim, p // (2 * xdim)] for p in range(2 * xdim * ZDIM)], axis=1
        )
        rt_gram = lax.dot_general(rt_half, rt_half, NT, preferred_element_type=F32)
        copies = []
        for h in range(PARTS):
            total = jnp.zeros((rank, part), F32)
            for i in range(local_runs):
                back = jnp.dot(rt_half, t_ref[i, :, h * part : (h + 1) * part], preferred_element_type=F32)
                total += back * jnp.concatenate([w_ref[i]] * (part // 128), axis=1)
            mzs[n, r, h] = total
            for d, q in enumerate(run_peers):
                copies.append(send(mzs.at[n, r, h], mzs.at[n, r, h], m_sem, (n, h, d), (q, s)))
        inverse = negative_inverse(run_gram * rt_gram)
        for copy in copies:
            copy.wait()
        for h in range(PARTS):
            total = mzs[n, 0, h]
            for d in range(1, runs):
                total += mzs[n, d, h]
            mz_ref[:, h * part : (h + 1) * part] = -jnp.dot(
                inverse, total, precision=HIGHEST, preferred_element_type=F32
            )
        return run_gram

    lax.fori_loop(0, SWEEPS, sweep, run_gram)
    mz_out[...] = mz_ref[...]


def shards(tensor, run_factor, mz_factor):
    runs, spec = lax.axis_size("run"), lax.axis_size("spec")
    xdim = spec // (2 * ZDIM)
    local_runs, rt_rows, mz_rows = tensor.shape
    rank = run_factor.shape[1]
    width = rt_rows // spec
    part = mz_rows // PARTS
    vmem = pl.BlockSpec(memory_space=pltpu.VMEM)
    square = (rank, rank)
    dma = pltpu.SemaphoreType.DMA
    near, far, line = max(xdim - 1, 1), ZDIM - 1, max(runs - 1, 1)
    rt_factor, mz_out = pl.pallas_call(
        functools.partial(kernel, runs, xdim),
        out_shape=(
            jax.ShapeDtypeStruct((rank, width), F32),
            jax.ShapeDtypeStruct((rank, mz_rows), F32),
        ),
        in_specs=[pl.BlockSpec(memory_space=pl.ANY), vmem, vmem, vmem],
        out_specs=(vmem, vmem),
        scratch_shapes=[
            pltpu.VMEM(tensor.shape, BF16),
            pltpu.VMEM((rank, mz_rows), F32),
            pltpu.VMEM((rank, mz_rows), BF16),
            pltpu.VMEM((local_runs, rank, 128), F32),
            pltpu.VMEM((runs, local_runs, rank), F32),
            pltpu.VMEM((SWEEPS,) + square, F32),
            pltpu.VMEM((SWEEPS, 2 * xdim - 1) + square, F32),
            pltpu.VMEM((SWEEPS,) + square, F32),
            pltpu.VMEM((SWEEPS, far) + square, F32),
            pltpu.VMEM((SWEEPS, 2, xdim, ZDIM, rank, width), F32),
            pltpu.VMEM((SWEEPS, xdim, ZDIM, rank, width), F32),
            pltpu.VMEM((SWEEPS, xdim, ZDIM, rank, width), F32),
            pltpu.VMEM((SWEEPS, near, ZDIM, rank, width), F32),
            pltpu.VMEM((SWEEPS, ZDIM, rank, width), F32),
            pltpu.VMEM((SWEEPS, far, rank, width), F32),
            pltpu.VMEM((SWEEPS, runs, rank, width), F32),
            pltpu.VMEM((SWEEPS, 2, xdim, ZDIM, rank, width), BF16),
            pltpu.VMEM((SWEEPS, runs, PARTS, rank, part), F32),
            dma,
            dma((2, line)),
            dma((2, SWEEPS, 2 * xdim - 1)),
            dma((2, SWEEPS, far)),
            dma((2, SWEEPS)),
            dma((2, SWEEPS, near)),
            dma((2, SWEEPS, far)),
            dma((2, SWEEPS, line)),
            dma((2, SWEEPS, far)),
            dma((2, SWEEPS, near)),
            dma((2, SWEEPS)),
            dma((2, SWEEPS, PARTS, line)),
        ],
        compiler_params=pltpu.CompilerParams(
            collective_id=0, has_side_effects=True, vmem_limit_bytes=56 * 1024 * 1024
        ),
    )(tensor, run_factor, run_factor.T, mz_factor.T)
    return rt_factor.T, mz_out.T


def solution(mesh):
    return jax.shard_map(
        shards,
        mesh=mesh,
        in_specs=(P("run", None, "spec"), P("run", None), P("spec", None)),
        out_specs=(P("spec", None), P("spec", None)),
        check_vma=False,
    )
```

```python
import functools

import jax
import jax.numpy as jnp
from jax import lax
from jax.experimental import pallas as pl
from jax.experimental.pallas import tpu as pltpu
from jax.sharding import PartitionSpec as P

SWEEPS = 3
ZDIM = 4
PARTS = 2
HIGHEST = lax.Precision.HIGHEST
F32 = jnp.float32
BF16 = jnp.bfloat16
NT = (((1,), (1,)), ((), ()))
TN = (((0,), (0,)), ((), ()))


def sweep_pairs(a, blocks):
    n = a.shape[0]
    lanes = lax.broadcasted_iota(jnp.int32, (1, n), 1)
    rows = lax.broadcasted_iota(jnp.int32, (n, 1), 0)

    def block(_, a):
        for p in range(0, 8, 2):
            q = p + 1
            c1 = jnp.broadcast_to(a[:, p : p + 1], (n, n))
            c2 = jnp.broadcast_to(a[:, q : q + 1], (n, n))
            b = c1[q : q + 1, :]
            inv = 1.0 / c1[p : p + 1, :]
            ratio = b * inv
            s22 = 1.0 / (c2[q : q + 1, :] - b * ratio)
            s12 = -ratio * s22
            s11 = inv - ratio * s12
            r1, r2 = a[p : p + 1, :], a[q : q + 1, :]
            h1, h2 = lanes == p, lanes == q
            m1 = jnp.where(h1, -s11, jnp.where(h2, -s12, s11 * r1 + s12 * r2))
            m2 = jnp.where(h1, -s12, jnp.where(h2, -s22, s12 * r1 + s22 * r2))
            swept = jnp.where(h1 | h2, 0.0, a) - c1 * m1 - c2 * m2
            a = jnp.where(rows == p, m1, jnp.where(rows == q, m2, swept))
        a = jnp.concatenate([a[8:], a[:8]], axis=0)
        return jnp.concatenate([a[:, 8:], a[:, :8]], axis=1)

    return lax.fori_loop(0, blocks, block, a)


def pack(g):
    half = g.shape[0] // 2
    return jnp.concatenate([g[:half], g[half:]], axis=1)


def unpack(g):
    half = g.shape[1] // 2
    return jnp.concatenate([g[:, :half], g[:, half:]], axis=0)


def kernel(
    runs, xdim, t_hbm, rf_ref, rft_ref, mz_in, rt_out, mz_out,
    t_ref, mz_ref, half_ref, w_ref, rf_all, gram_own, gram_a, gram_sum, gram_b,
    mom, mom_c, red_c, mom_x, red_x, mom_zr, rt_all, mzs, inv_ref,
    load_sem, rf_sem, ga_sem, gb_sem, c_sem, x_sem, zr_sem, az_sem, ax_sem, m_sem,
):
    r = lax.axis_index("run")
    s = lax.axis_index("spec")
    c = lax.rem(s, 2)
    x = lax.rem(s // 2, xdim)
    z = s // (2 * xdim)
    local_runs, width = t_ref.shape[0], rt_out.shape[1]
    rank, mz_rows = mz_in.shape
    part = mz_rows // PARTS

    load = pltpu.make_async_copy(t_hbm, t_ref, load_sem)
    load.start()

    core_peer = s + 1 - 2 * c
    x_peers = [(lax.rem(x + d, xdim) - x) * 2 + s for d in range(1, xdim)]
    z_peers = [(lax.rem(z + d, ZDIM) - z) * 2 * xdim + s for d in range(1, ZDIM)]
    run_peers = [lax.rem(r + d, runs) for d in range(1, runs)]
    inner = lax.rem(s, 2 * xdim)
    inner_peers = [s - inner + lax.rem(inner + d, 2 * xdim) for d in range(1, 2 * xdim)]

    zr_peers = []
    for e in range(runs):
        for d in range(ZDIM):
            if e or d:
                zz = lax.rem(z + d, ZDIM)
                zr_peers.append((zz, (lax.rem(r + e, runs), s + (zz - z) * 2 * xdim)))

    everyone = [(r, q) for q in inner_peers] + [peer for _, peer in zr_peers]
    barrier = pltpu.get_barrier_semaphore()
    for peer in everyone:
        pl.semaphore_signal(barrier, inc=1, device_id=peer, device_id_type=pl.DeviceIdType.MESH)
    pl.semaphore_wait(barrier, len(everyone))

    def send(src, dst, sems, index, peer):
        copy = pltpu.make_async_remote_copy(
            src_ref=src, dst_ref=dst, send_sem=sems.at[(0,) + index], recv_sem=sems.at[(1,) + index],
            device_id=peer, device_id_type=pl.DeviceIdType.MESH,
        )
        copy.start()
        return copy

    rf_all[r] = rf_ref[...]
    rf_copies = [send(rf_all.at[r], rf_all.at[r], rf_sem, (d,), (q, s)) for d, q in enumerate(run_peers)]
    mz_ref[...] = mz_in[...]
    for i in range(local_runs):
        w_ref[i] = jnp.broadcast_to(rft_ref[:, i : i + 1], w_ref.shape[1:])
    for copy in rf_copies:
        copy.wait()
    run_gram = jnp.zeros((rank, rank), F32)
    for i in range(runs):
        run_gram += lax.dot_general(rf_all[i], rf_all[i], TN, precision=HIGHEST, preferred_element_type=F32)
    load.wait()

    def sweep(n, run_gram):
        mz_now = mz_ref[...]
        gram = lax.dot_general(mz_now, mz_now, NT, precision=HIGHEST, preferred_element_type=F32)
        gram_own[n] = pack(gram)
        ga = [send(gram_own.at[n], gram_a.at[n, d], ga_sem, (n, d), (r, q)) for d, q in enumerate(inner_peers)]
        half_ref[...] = mz_now.astype(BF16)

        def project(cc, xx):
            for zz in range(0, ZDIM, 2):
                total = jnp.zeros((rank, 2 * width), F32)
                starts = [pl.multiple_of((((zz + e) * xdim + xx) * 2 + cc) * width, width) for e in range(2)]
                for i in range(local_runs):
                    slab = jnp.concatenate([t_ref[i, pl.ds(at, width), :] for at in starts], axis=0)
                    proj = lax.dot_general(half_ref[...], slab, NT, preferred_element_type=F32)
                    total += proj * jnp.concatenate([w_ref[i][:, :width]] * 2, axis=1)
                mom[n, cc, xx, zz] = total[:, :width]
                mom[n, cc, xx, zz + 1] = total[:, width:]

        for xx in range(xdim):
            project(1 - c, xx)
        to_core = send(mom.at[n, 1 - c], mom_c.at[n], c_sem, (n,), (r, core_peer))
        others = [lax.rem(x + d, xdim) for d in range(1, xdim)]
        for xx in others:
            project(c, xx)
        for copy in ga:
            copy.wait()
        total = gram_own[n]
        for d in range(len(ga)):
            total += gram_a[n, d]
        gram_sum[n] = total
        gb = [send(gram_sum.at[n], gram_b.at[n, d], gb_sem, (n, d), (r, q)) for d, q in enumerate(z_peers)]
        to_core.wait()
        to_x = []
        for d, xx in enumerate(others):
            red_c[n, xx] = mom[n, c, xx] + mom_c[n, xx]
            to_x.append(send(red_c.at[n, xx], mom_x.at[n, d], x_sem, (n, d), (r, x_peers[d])))
        project(c, x)
        for copy in gb:
            copy.wait()
        total = gram_sum[n]
        for d in range(len(gb)):
            total += gram_b[n, d]
        inv_ref[...] = sweep_pairs(run_gram * unpack(total), rank // 16)
        for copy in to_x:
            copy.wait()
        total = mom[n, c, x] + mom_c[n, x]
        for d in range(len(to_x)):
            total += mom_x[n, d]
        red_x[n] = total
        to_zr = [
            send(red_x.at[n, zz], mom_zr.at[n, r, z], zr_sem, (n, d), peer)
            for d, (zz, peer) in enumerate(zr_peers)
        ]
        mom_zr[n, r, z] = red_x[n, z]
        inv_ref[...] = sweep_pairs(inv_ref[...], rank // 16)
        for copy in to_zr:
            copy.wait()
        total = jnp.zeros((rank, width), F32)
        for e in range(runs):
            for d in range(ZDIM):
                total += mom_zr[n, e, d]
        rt = -jnp.dot(inv_ref[...], total, precision=HIGHEST, preferred_element_type=F32)
        rt_out[...] = rt

        rt_all[n, c, x, z] = rt.astype(BF16)
        own = rt_all.at[n, c, x, z]
        copies = [send(own, own, az_sem, (n, d), (r, q)) for d, q in enumerate(z_peers)]
        for copy in copies:
            copy.wait()
        own = rt_all.at[n, c, x]
        copies = [send(own, own, ax_sem, (n, d), (r, q)) for d, q in enumerate(inner_peers)]
        for copy in copies:
            copy.wait()
        rt_half = jnp.concatenate(
            [rt_all[n, p % 2, p // 2 % xdim, p // (2 * xdim)] for p in range(2 * xdim * ZDIM)], axis=1
        )
        rt_gram = lax.dot_general(rt_half, rt_half, NT, preferred_element_type=F32)
        copies = []
        for h in range(PARTS):
            total = jnp.zeros((rank, part), F32)
            for i in range(local_runs):
                back = jnp.dot(rt_half, t_ref[i, :, h * part : (h + 1) * part], preferred_element_type=F32)
                total += back * jnp.concatenate([w_ref[i]] * (part // 128), axis=1)
            mzs[n, r, h] = total
            for d, q in enumerate(run_peers):
                copies.append(send(mzs.at[n, r, h], mzs.at[n, r, h], m_sem, (n, h, d), (q, s)))
        inv_ref[...] = sweep_pairs(run_gram * rt_gram, rank // 8)
        for copy in copies:
            copy.wait()
        for h in range(PARTS):
            total = mzs[n, 0, h]
            for d in range(1, runs):
                total += mzs[n, d, h]
            mz_ref[:, h * part : (h + 1) * part] = -jnp.dot(
                inv_ref[...], total, precision=HIGHEST, preferred_element_type=F32
            )
        return run_gram

    lax.fori_loop(0, SWEEPS, sweep, run_gram)
    mz_out[...] = mz_ref[...]


def shards(tensor, run_factor, mz_factor):
    runs, spec = lax.axis_size("run"), lax.axis_size("spec")
    xdim = spec // (2 * ZDIM)
    local_runs, rt_rows, mz_rows = tensor.shape
    rank = run_factor.shape[1]
    width = rt_rows // spec
    part = mz_rows // PARTS
    vmem = pl.BlockSpec(memory_space=pltpu.VMEM)
    square, packed = (rank, rank), (rank // 2, 2 * rank)
    dma = pltpu.SemaphoreType.DMA
    near, far, line = max(xdim - 1, 1), ZDIM - 1, max(runs - 1, 1)
    rt_factor, mz_out = pl.pallas_call(
        functools.partial(kernel, runs, xdim),
        out_shape=(
            jax.ShapeDtypeStruct((rank, width), F32),
            jax.ShapeDtypeStruct((rank, mz_rows), F32),
        ),
        in_specs=[pl.BlockSpec(memory_space=pl.ANY), vmem, vmem, vmem],
        out_specs=(vmem, vmem),
        scratch_shapes=[
            pltpu.VMEM(tensor.shape, BF16),
            pltpu.VMEM((rank, mz_rows), F32),
            pltpu.VMEM((rank, mz_rows), BF16),
            pltpu.VMEM((local_runs, rank, 128), F32),
            pltpu.VMEM((runs, local_runs, rank), F32),
            pltpu.VMEM((SWEEPS,) + packed, F32),
            pltpu.VMEM((SWEEPS, 2 * xdim - 1) + packed, F32),
            pltpu.VMEM((SWEEPS,) + packed, F32),
            pltpu.VMEM((SWEEPS, far) + packed, F32),
            pltpu.VMEM((SWEEPS, 2, xdim, ZDIM, rank, width), F32),
            pltpu.VMEM((SWEEPS, xdim, ZDIM, rank, width), F32),
            pltpu.VMEM((SWEEPS, xdim, ZDIM, rank, width), F32),
            pltpu.VMEM((SWEEPS, near, ZDIM, rank, width), F32),
            pltpu.VMEM((SWEEPS, ZDIM, rank, width), F32),
            pltpu.VMEM((SWEEPS, runs, ZDIM, rank, width), F32),
            pltpu.VMEM((SWEEPS, 2, xdim, ZDIM, rank, width), BF16),
            pltpu.VMEM((SWEEPS, runs, PARTS, rank, part), F32),
            pltpu.VMEM(square, F32),
            dma,
            dma((2, line)),
            dma((2, SWEEPS, 2 * xdim - 1)),
            dma((2, SWEEPS, far)),
            dma((2, SWEEPS)),
            dma((2, SWEEPS, near)),
            dma((2, SWEEPS, runs * ZDIM - 1)),
            dma((2, SWEEPS, far)),
            dma((2, SWEEPS, 2 * xdim - 1)),
            dma((2, SWEEPS, PARTS, line)),
        ],
        compiler_params=pltpu.CompilerParams(
            collective_id=0, has_side_effects=True, vmem_limit_bytes=56 * 1024 * 1024
        ),
    )(tensor, run_factor, run_factor.T, mz_factor.T)
    return rt_factor.T, mz_out.T


def solution(mesh):
    return jax.shard_map(
        shards,
        mesh=mesh,
        in_specs=(P("run", None, "spec"), P("run", None), P("spec", None)),
        out_specs=(P("spec", None), P("spec", None)),
        check_vma=False,
    )
```
